1024 devices in a mesh: node: 32 (over z_hi, x, core), local: 32 (over z_lo, y).
Axes of the slice: x: 4, y: 4, z: 32 (z_hi: 4, z_lo: 8; z = z_hi * 8 + z_lo), core: 2. Of those that a mesh axis runs over, the one named last changes fastest.
Arguments:
- d_out: bfloat16 [4096, 7168], P('node', 'local'), may hold values from -6 to 6
- combine: float32 [4096, 3], P('node'), may hold values from 0.05 to 1
- expert_ids: int32 [4096, 3], P('node'), may hold values from 0 to 31, as said below
- slot_ids: int32 [4096, 3], P('node'), may hold values from -1 to 11, as said below
- w_gate: bfloat16 [32, 7168, 2048], P('node', 'local'), may hold values from -0.0625 to 0.0625
- w_up: bfloat16 [32, 7168, 2048], P('node', 'local'), may hold values from -0.0625 to 0.0625
- w_down: bfloat16 [32, 2048, 7168], P('node', None, 'local'), may hold values from -0.125 to 0.125
- saved_gate: bfloat16 [32, 384, 2048], P('node'), may hold values from -6 to 6
- saved_up: bfloat16 [32, 384, 2048], P('node'), may hold values from -6 to 6
Outputs:
- d_input: bfloat16 [4096, 7168], P('node', 'local')
The draws below stay inside these ranges and needn't reach their ends.
Inputs may be any that keep to these rules, and one draw needn't show every extreme that they name: `expert_ids`: each token names 3 different experts. `slot_ids`: picks of one source node at one expert hold distinct slots, numbered in the order of the tokens; -1 marks a pick beyond the 12 rows of that block, which is dropped; in every draw some source node fills all 12 rows at some expert.
All inputs are finite; a program needn't handle non-finite values.
Results may differ from the reference program's by a relative error of at most 0.034.
Values may be sent and summed in bfloat16 or wider, within the bound.
A program may use at most 32 MiB of HBM per device.

```python
import jax
import jax.numpy as jnp
from jax import lax

D = 7168
HID = 2048
TOK_NODE = 128
TOPK = 3
EXPERTS = 32
CAPN = 12
TOKENS = 4096
N_NODE = 32
N_LOCAL = 32


def routing(key):
    baseline_score = jax.random.randint(jax.random.fold_in(key, 11), (N_NODE, TOK_NODE, N_NODE), 0, 65536)
    preference_boost = jax.random.randint(jax.random.fold_in(key, 12), (N_NODE, 1, N_NODE), 0, 32768)
    busiest_node = jax.random.randint(jax.random.fold_in(key, 13), (N_NODE, 1, 1), 0, N_NODE)
    perm_keys = jax.random.split(jax.random.fold_in(key, 14), N_NODE)
    perms = jax.vmap(lambda one_key: jax.random.permutation(one_key, TOK_NODE))(perm_keys)
    position = jnp.argsort(perms, axis=1, stable=True)
    selected_node = position < min(2 * CAPN, TOK_NODE)
    target_node_index = jnp.arange(N_NODE, dtype=jnp.int32)[None, None, :]
    extra_credit = jnp.where(selected_node[:, :, None] & (target_node_index == busiest_node), 1048576, 0)
    node_score = (baseline_score + preference_boost + extra_credit) * N_NODE + target_node_index
    _, picks = lax.top_k(node_score, TOPK)
    picks = picks.astype(jnp.int32)
    onehot = (picks[..., None] == target_node_index[:, :, None, :]).astype(jnp.int32)
    count = jnp.sum(onehot, axis=2)
    rank = jnp.cumsum(count, axis=1) - count
    slots = jnp.sum(onehot * rank[:, :, None, :], axis=3)
    slots = jnp.where(slots < CAPN, slots, -1).astype(jnp.int32)
    return (picks.reshape(TOKENS, TOPK), slots.reshape(TOKENS, TOPK))


def draw_expert_ids(key, part):
    return routing(key)[0]


def draw_slot_ids(key, part):
    return routing(key)[1]


def steps_of(key, extent, cuts, low, top_value):
    def one(dim, parts):
        heights = jax.random.uniform(jax.random.fold_in(jax.random.fold_in(key, 6), dim), (parts,), jnp.float32, low / len(cuts), top_value / len(cuts))
        return jnp.repeat(jnp.exp(heights), extent[dim] // parts).reshape((-1,) + (1,) * (len(extent) - dim - 1))

    gain = one(*cuts[0])
    for cut in cuts[1:]:
        gain = gain * one(*cut)
    return gain


def bell_draw(own_key, extent, deviation, limit, cuts=(), held_as=jnp.bfloat16):
    level = steps_of(own_key, extent, cuts, -0.22, 0.18) if cuts else 1.0
    entries = jax.random.normal(own_key, extent, jnp.float32) * deviation * level
    return jnp.minimum(jnp.maximum(entries, -limit), limit).astype(held_as)


def setup_inputs(seed: int = 0) -> dict:
    keys = jax.random.split(jax.random.key(seed), 10)
    return {
        "d_out": bell_draw(keys[0], (TOKENS, D), 1.0, 6.0, ((0, 32), (1, 32))),
        "combine": jnp.clip(0.05 + 0.95 * jax.random.uniform(keys[1], (TOKENS, TOPK), jnp.float32) ** steps_of(keys[1], (TOKENS, TOPK), ((0, 32),), -0.2, 0.2), 0.05, 1.0),
        "expert_ids": draw_expert_ids(jax.random.fold_in(keys[9], 71), 0),
        "slot_ids": draw_slot_ids(jax.random.fold_in(keys[9], 71), 0),
        "w_gate": bell_draw(keys[4], (EXPERTS, D, HID), D ** -0.5, 0.0625, ((0, 32), (1, 32))),
        "w_up": bell_draw(keys[5], (EXPERTS, D, HID), D ** -0.5, 0.0625, ((0, 32), (1, 32))),
        "w_down": bell_draw(keys[6], (EXPERTS, HID, D), HID ** -0.5, 0.125, ((0, 32), (2, 32))),
        "saved_gate": bell_draw(keys[7], (EXPERTS, N_NODE * CAPN, HID), 1.0, 6.0, ((0, 32),)),
        "saved_up": bell_draw(keys[8], (EXPERTS, N_NODE * CAPN, HID), 1.0, 6.0, ((0, 32),)),
    }


def swiglu_back(grad_hidden, gate_value, up_value):
    gate_float = gate_value.astype(jnp.float32)
    up_float = up_value.astype(jnp.float32)
    sigmoid_gate = jax.nn.sigmoid(gate_float)
    grad_gate = grad_hidden * up_float * sigmoid_gate * (1.0 + gate_float * (1.0 - sigmoid_gate))
    grad_up = grad_hidden * gate_float * sigmoid_gate
    return grad_gate.astype(jnp.bfloat16), grad_up.astype(jnp.bfloat16)


def slot_layout(expert_rows, slot_rows):
    slot_total = N_NODE * CAPN
    is_kept = slot_rows >= 0
    slot_place = jnp.where(is_kept, expert_rows * CAPN + slot_rows, slot_total).astype(jnp.int32)
    return is_kept, slot_place


def send_block(inputs):
    d_rows, weights, expert_rows, slot_rows = inputs
    slot_total = N_NODE * CAPN
    is_kept, slot_place = slot_layout(expert_rows, slot_rows)
    token_index = jnp.broadcast_to(jnp.arange(TOK_NODE, dtype=jnp.int32)[:, None], slot_place.shape)
    slot_owner = jnp.zeros((slot_total + 1,), jnp.int32).at[slot_place.reshape(-1)].set(token_index.reshape(-1))[:slot_total]
    slot_weight = jnp.zeros((slot_total + 1,), jnp.float32).at[slot_place.reshape(-1)].set(weights.reshape(-1))[:slot_total]
    scaled = (d_rows[slot_owner].astype(jnp.float32) * slot_weight[:, None]).astype(jnp.bfloat16)
    return scaled.reshape(N_NODE, CAPN, D)


def expert_back(inputs):
    arrived, gate_weight, up_weight, down_weight, gate_saved, up_saved = inputs
    feat_block = D // N_LOCAL
    row_count = N_NODE * CAPN
    row_blocks = jnp.moveaxis(arrived.astype(jnp.float32).reshape(row_count, N_LOCAL, feat_block), 1, 0)
    down_blocks = jnp.moveaxis(down_weight.astype(jnp.float32).reshape(HID, N_LOCAL, feat_block), 1, 0)

    def add_block(running, block_pair):
        row_part, down_part = block_pair
        block_part = jnp.dot(row_part, down_part.T, preferred_element_type=jnp.float32, precision=lax.Precision.HIGHEST)
        block_part = lax.optimization_barrier(block_part.astype(jnp.bfloat16)).astype(jnp.float32)
        return running + block_part, None

    grad_hidden, _ = lax.scan(add_block, jnp.zeros((row_count, HID), jnp.float32), (row_blocks, down_blocks))
    grad_gate, grad_up = swiglu_back(grad_hidden, gate_saved, up_saved)
    grad_rows = jnp.dot(grad_gate.astype(jnp.float32), gate_weight.astype(jnp.float32).T, preferred_element_type=jnp.float32, precision=lax.Precision.HIGHEST)
    grad_rows = grad_rows + jnp.dot(grad_up.astype(jnp.float32), up_weight.astype(jnp.float32).T, preferred_element_type=jnp.float32, precision=lax.Precision.HIGHEST)
    return grad_rows.astype(jnp.bfloat16)


def collect(inputs):
    back_rows, expert_rows, slot_rows = inputs
    is_kept, slot_place = slot_layout(expert_rows, slot_rows)
    flat_rows = back_rows.reshape(N_NODE * CAPN, D)
    pick_index = jnp.where(is_kept, slot_place, 0).astype(jnp.int32)
    picked = flat_rows[pick_index].astype(jnp.float32) * is_kept[..., None].astype(jnp.float32)
    return jnp.sum(picked, axis=1).astype(jnp.bfloat16)


def reference(d_out, combine, expert_ids, slot_ids, w_gate, w_up, w_down, saved_gate, saved_up):
    expert_blocks = expert_ids.reshape(N_NODE, TOK_NODE, TOPK)
    slot_blocks = slot_ids.reshape(N_NODE, TOK_NODE, TOPK)
    blocks = (d_out.reshape(N_NODE, TOK_NODE, D), combine.reshape(N_NODE, TOK_NODE, TOPK), expert_blocks, slot_blocks)
    outgoing = lax.map(send_block, blocks)
    arrived = jnp.swapaxes(outgoing, 0, 1).reshape(N_NODE, N_NODE * CAPN, D)
    grad_rows = lax.map(expert_back, (arrived, w_gate, w_up, w_down, saved_gate, saved_up))
    back_rows = jnp.swapaxes(grad_rows.reshape(N_NODE, N_NODE, CAPN, D), 0, 1)
    d_input = lax.map(collect, (back_rows, expert_blocks, slot_blocks))
    return d_input.reshape(TOKENS, D)
```

```python
import functools

import jax
import jax.numpy as jnp
import numpy as np
from jax import lax
from jax.experimental import pallas as pl
from jax.experimental.pallas import tpu as pltpu
from jax.sharding import PartitionSpec as P

F32, BF16 = jnp.float32, jnp.bfloat16
GROUPS, PEERS, CAP = 4, 8, 12
ROWS = PEERS * CAP
PART = GROUPS * CAP
SLOTS = GROUPS * ROWS
ORDER = (0, 1, 3, 2)
LAG = (0, 3, 4, 7)
STAGES = 11
NCOPY = 3 + 7 + 3 + 7 + GROUPS * 14


def mul(value, unit):
    return pl.multiple_of(value, unit)


def contract(a, b):
    return lax.dot_general(a, b, (((1,), (1,)), ((), ())), preferred_element_type=F32)


def kernel(
    d_out, place_row, weight_row, place_col, perm_out, perm_back, wg_hbm, wu_hbm, wd_hbm, sg_hbm, su_hbm,
    result,
    wg, wu, wd, sg, su, fac_g, fac_u, out, x1, zsend, arr, part, r1, ys2, t2, r2, zs1, z1, u1, zs2, z2, u2, zs3, z3, u3,
    dh, gr, ret, snd, rx, pick, load_sem, send_sem, recv_sem,
):
    hid, feat = wd.shape
    node, local = lax.axis_index("node"), lax.axis_index("local")
    zh, j = lax.div(node, PEERS), lax.rem(node, PEERS)
    zl, y = lax.div(local, 4), lax.rem(local, 4)
    ya = y + 1 - 2 * lax.rem(y, 2)
    yb = 3 - y
    b0, b1, b2 = lax.rem(zl, 2), lax.rem(lax.div(zl, 2), 2), lax.div(zl, 4)
    to_z1, to_z2, to_z3 = zl + 1 - 2 * b0, zl + 2 - 4 * b1, zl + 4 - 8 * b2
    half = (lax.rem(lax.div(y + 1, 2), 2), lax.div(y, 2))
    quarter = (lax.div(y, 2), lax.rem(y, 2))
    first_to, second_to = (ya, yb), (yb, ya)
    own1 = [s * (hid // 2) + half[s] * (hid // 4) for s in range(2)]
    other1 = [s * (hid // 2) + (1 - half[s]) * (hid // 4) for s in range(2)]
    own2 = [own1[s] + quarter[s] * (hid // 8) for s in range(2)]
    other2 = [own1[s] + (1 - quarter[s]) * (hid // 8) for s in range(2)]
    own3 = own2[0] + b0 * (own2[1] - own2[0])
    own4 = own3 + b1 * (hid // 16)
    w4, w8, w16 = hid // 4, hid // 8, hid // 16

    def cols(start, size):
        return pl.ds(mul(start, 128), size)

    def peer(k):
        return {"node": zh * PEERS + k, "local": local}

    def group(k):
        return {"node": k * PEERS + j, "local": local}

    def at_y(k):
        return {"node": node, "local": zl * 4 + k}

    def at_z(k):
        return {"node": node, "local": k * 4 + y}

    loads = [
        pltpu.make_async_copy(src, dst, load_sem.at[i])
        for i, (src, dst) in enumerate(((wd_hbm, wd), (sg_hbm, sg), (su_hbm, su), (wg_hbm, wg), (wu_hbm, wu)))
    ]
    for load in loads:
        load.start()

    barrier = pltpu.get_barrier_semaphore()
    partners = [peer(lax.rem(j + o, PEERS)) for o in range(1, PEERS)]
    partners += [group(lax.rem(zh + d, GROUPS)) for d in range(1, GROUPS)]
    partners += [at_y(ya), at_y(yb), at_z(to_z1), at_z(to_z2), at_z(to_z3)]
    for partner in partners:
        pl.semaphore_signal(barrier, inc=1, device_id=partner, device_id_type=pl.DeviceIdType.MESH)

    slot = lax.broadcasted_iota(jnp.int32, (SLOTS, d_out.shape[0]), 0)
    chosen = jnp.zeros(slot.shape, F32)
    weight = jnp.zeros(slot.shape, F32)
    for k in range(3):
        hit = slot == place_row[k : k + 1, :]
        chosen = chosen + jnp.where(hit, 1.0, 0.0)
        weight = weight + jnp.where(hit, weight_row[k : k + 1, :], 0.0)
    weight = jnp.sum(weight, axis=1, keepdims=True)
    rows = jnp.dot(chosen.astype(BF16), d_out[...], preferred_element_type=F32)
    out[...] = (rows * weight).astype(BF16)

    pl.semaphore_wait(barrier, len(partners))

    started = []

    def send(src, dst, to):
        i = len(started)
        copy = pltpu.make_async_remote_copy(
            src_ref=src, dst_ref=dst, send_sem=send_sem.at[i], recv_sem=recv_sem.at[i],
            device_id=to, device_id_type=pl.DeviceIdType.MESH,
        )
        copy.start()
        started.append(copy)
        return copy

    def piece(k):
        return pl.ds(mul(k * PART, 16), PART)

    to_peers = [
        send(out.at[piece(lax.rem(j + o, PEERS))], x1.at[piece(j)], peer(lax.rem(j + o, PEERS)))
        for o in range(1, PEERS)
    ]
    x1[piece(j), :] = out[piece(j), :]
    where = lax.broadcasted_iota(jnp.int32, pick.shape, 1)
    picked = jnp.zeros(pick.shape, F32)
    for k in range(3):
        picked = picked + jnp.where(where == place_col[:, k : k + 1], 1.0, 0.0)
    pick[...] = picked.astype(BF16)
    for copy in to_peers:
        copy.wait_recv()
    sorted_rows = jnp.dot(perm_out[...], x1[...], preferred_element_type=F32).astype(BF16)
    for d in range(GROUPS):
        block = sorted_rows[d * ROWS : (d + 1) * ROWS]
        if d == 0:
            arr[0] = block
        else:
            zsend[d] = block
    to_groups = {}
    for d in ORDER[1:]:
        to_groups[d] = send(zsend.at[d], arr.at[d], group(lax.rem(zh + d, GROUPS)))
    loads[0].wait()

    def factors(d):
        base = lax.rem(zh - d + GROUPS, GROUPS) * ROWS

        def step(i, carry):
            r = pl.ds(mul(base + i * 16, 16), 16)
            gate, up = sg[r, :].astype(F32), su[r, :].astype(F32)
            sig = 1.0 / (1.0 + jnp.exp(-gate))
            to = pl.ds(mul(i * 16, 16), 16)
            fac_g[d, to, :] = up * sig * (1.0 + gate * (1.0 - sig))
            fac_u[d, to, :] = gate * sig
            return carry

        lax.fori_loop(0, ROWS // 16, step, 0)

    pending = {}
    returned = {}

    def stage(d, s):
        if s == 0:
            if d:
                to_groups[d].wait_recv()

            def mat(i, carry):
                c = cols(i * w4, w4)
                part[d, :, c] = contract(arr[d], wd[pl.ds(mul(i * w4, 128), w4), :]).astype(BF16)
                return carry

            lax.fori_loop(0, 4, mat, 0)
            pending[d] = [send(part.at[d, :, cols(other1[k], w4)], r1.at[d, k], at_y(first_to[k])) for k in range(2)]
            if d == 0:
                loads[1].wait()
                loads[2].wait()
            factors(d)
            return
        for copy in pending[d]:
            copy.wait_recv()
        if s == 1:
            pending[d] = []
            for k in range(2):
                ys2[d, k] = (
                    part[d, :, cols(other2[k], w8)].astype(F32)
                    + r1[d, k, :, cols((1 - quarter[k]) * w8, w8)].astype(F32)
                ).astype(BF16)
                pending[d].append(send(ys2.at[d, k], r2.at[d, k], at_y(second_to[k])))
            for k in range(2):
                t2[d, k] = part[d, :, cols(own2[k], w8)].astype(F32) + r1[d, k, :, cols(quarter[k] * w8, w8)].astype(F32)
        elif s == 2:
            zs1[d] = (t2[d, 1 - b0] + r2[d, 1 - b0].astype(F32)).astype(BF16)
            pending[d] = [send(zs1.at[d], z1.at[d], at_z(to_z1))]
            u1[d] = t2[d, b0] + r2[d, b0].astype(F32)
        elif s == 3:
            far, near = cols((1 - b1) * w16, w16), cols(b1 * w16, w16)
            zs2[d] = (u1[d, :, far] + z1[d, :, far].astype(F32)).astype(BF16)
            pending[d] = [send(zs2.at[d], z2.at[d], at_z(to_z2))]
            u2[d] = u1[d, :, near] + z1[d, :, near].astype(F32)
        elif s == 4:
            far, near = pl.ds(mul((1 - b2) * 48, 16), 48), pl.ds(mul(b2 * 48, 16), 48)
            zs3[d] = (u2[d, far, :] + z2[d, far, :].astype(F32)).astype(BF16)
            pending[d] = [send(zs3.at[d], z3.at[d], at_z(to_z3))]
            u3[d] = u2[d, near, :] + z2[d, near, :].astype(F32)
        elif s == 5:
            r, c = pl.ds(mul(b2 * 48, 16), 48), cols(own4, w16)
            dh[d, r, c] = (u3[d] + z3[d].astype(F32)).astype(BF16)
            ref = dh.at[d, r, c]
            pending[d] = [send(ref, ref, at_z(to_z3))]
        elif s == 6:
            ref = dh.at[d, :, cols(own4, w16)]
            pending[d] = [send(ref, ref, at_z(to_z2))]
        elif s == 7:
            ref = dh.at[d, :, cols(own3, w8)]
            pending[d] = [send(ref, ref, at_z(to_z1))]
        elif s == 8:
            refs = [dh.at[d, :, cols(own2[k], w8)] for k in range(2)]
            pending[d] = [send(refs[k], refs[k], at_y(second_to[k])) for k in range(2)]
        elif s == 9:
            refs = [dh.at[d, :, cols(own1[k], w4)] for k in range(2)]
            pending[d] = [send(refs[k], refs[k], at_y(first_to[k])) for k in range(2)]
        else:
            if d == 0:
                loads[3].wait()
                loads[4].wait()

            def mat(i, total):
                c = cols(i * w4, w4)
                grad = dh[d, :, c].astype(F32)
                total = total + contract((grad * fac_g[d, :, c]).astype(BF16), wg[:, c])
                return total + contract((grad * fac_u[d, :, c]).astype(BF16), wu[:, c])

            total = lax.fori_loop(0, 4, mat, jnp.zeros((ROWS, feat), F32)).astype(BF16)
            if d == 0:
                ret[pl.ds(0, ROWS), :] = total
            else:
                gr[d] = total
                returned[d] = send(
                    gr.at[d], ret.at[pl.ds(d * ROWS, ROWS)], group(lax.rem(zh - d + GROUPS, GROUPS))
                )

    for t in range(max(LAG) + STAGES):
        for k, d in enumerate(ORDER):
            if 0 <= t - LAG[k] < STAGES:
                stage(d, t - LAG[k])

    for d in ORDER[1:]:
        returned[d].wait_recv()
    snd[...] = jnp.dot(perm_back[...], ret[...], preferred_element_type=F32).astype(BF16)
    to_peers = [
        send(snd.at[piece(lax.rem(j + o, PEERS))], rx.at[piece(j)], peer(lax.rem(j + o, PEERS)))
        for o in range(1, PEERS)
    ]
    rx[piece(j), :] = snd[piece(j), :]
    for copy in to_peers:
        copy.wait_recv()
    result[...] = jnp.dot(pick[...], rx[...], preferred_element_type=F32).astype(BF16)
    for copy in started:
        copy.wait_send()


def on_device(d_out, combine, expert_ids, slot_ids, w_gate, w_up, w_down, saved_gate, saved_up):
    feat, hid = w_gate.shape[1:]
    zh = lax.axis_index("node") // PEERS
    distance = (expert_ids // PEERS - zh + GROUPS) % GROUPS
    place = jnp.where(slot_ids >= 0, (expert_ids % PEERS) * PART + distance * CAP + slot_ids, 2 * SLOTS)
    r = np.arange(SLOTS)
    peer, rest = r // PART, r % PART
    target = (rest // CAP) * ROWS + peer * CAP + rest % CAP
    back = np.zeros((SLOTS, SLOTS), np.float32)
    back[r, target] = 1.0
    perm_back = jnp.asarray(back, BF16)
    perm_out = jnp.asarray(back.T, BF16)

    def two(*shape):
        return pltpu.VMEM(shape, BF16)

    def four(*shape):
        return pltpu.VMEM(shape, F32)

    vmem = pl.BlockSpec(memory_space=pltpu.VMEM)
    hbm = pl.BlockSpec(memory_space=pl.ANY)
    g = GROUPS
    return pl.pallas_call(
        kernel,
        out_shape=jax.ShapeDtypeStruct(d_out.shape, BF16),
        in_specs=[vmem] * 6 + [hbm] * 5,
        out_specs=vmem,
        scratch_shapes=[
            two(feat, hid), two(feat, hid), two(hid, feat), two(SLOTS, hid), two(SLOTS, hid),
            four(g, ROWS, hid), four(g, ROWS, hid),
            two(SLOTS, feat), two(SLOTS, feat), two(g, ROWS, feat), two(g, ROWS, feat),
            two(g, ROWS, hid), two(g, 2, ROWS, hid // 4), two(g, 2, ROWS, hid // 8), four(g, 2, ROWS, hid // 8),
            two(g, 2, ROWS, hid // 8), two(g, ROWS, hid // 8), two(g, ROWS, hid // 8), four(g, ROWS, hid // 8),
            two(g, ROWS, hid // 16), two(g, ROWS, hid // 16), four(g, ROWS, hid // 16),
            two(g, ROWS // 2, hid // 16), two(g, ROWS // 2, hid // 16), four(g, ROWS // 2, hid // 16),
            two(g, ROWS, hid), two(g, ROWS, feat), two(SLOTS, feat), two(SLOTS, feat), two(SLOTS, feat),
            two(d_out.shape[0], SLOTS),
            pltpu.SemaphoreType.DMA((5,)), pltpu.SemaphoreType.DMA((NCOPY,)), pltpu.SemaphoreType.DMA((NCOPY,)),
        ],
        compiler_params=pltpu.CompilerParams(
            collective_id=0, has_side_effects=True, vmem_limit_bytes=48 * 1024 * 1024
        ),
        cost_estimate=pl.CostEstimate(flops=1_200_000_000, bytes_accessed=8_000_000, transcendentals=800_000),
    )(
        d_out, place.T, combine.T, place, perm_out, perm_back,
        w_gate[0], w_up[0], w_down[0], saved_gate[0], saved_up[0],
    )


def solution(mesh):
    return jax.shard_map(
        on_device,
        mesh=mesh,
        in_specs=(
            P("node", "local"), P("node", None), P("node", None), P("node", None),
            P("node", "local", None), P("node", "local", None), P("node", None, "local"),
            P("node", None, None), P("node", None, None),
        ),
        out_specs=P("node", "local"),
        check_vma=False,
    )
```

```python
import jax
import jax.numpy as jnp
from jax import lax
from jax.experimental import pallas as pl
from jax.experimental.pallas import tpu as pltpu
from jax.sharding import PartitionSpec as P

F32, BF16 = jnp.float32, jnp.bfloat16
GROUPS, PEERS, CAP = 4, 8, 12
ROWS = PEERS * CAP
PART = GROUPS * CAP
SLOTS = GROUPS * ROWS
ORDER = (0, 1, 3, 2)
LAG = (0, 2, 2, 3)
STAGES = 6
NCOPY = 2 * 7 + 2 * 3 + 3 * 3 + GROUPS * 13
MESH = pl.DeviceIdType.MESH


def mul(value, unit):
    return pl.multiple_of(value, unit)


def mat(a, b):
    return jnp.dot(a, b, preferred_element_type=F32)


def contract(a, b, dim):
    return lax.dot_general(a, b, (((dim,), (dim,)), ((), ())), preferred_element_type=F32)


def by_const(value, factor):
    return lax.shift_right_logical(value * factor, jnp.full(value.shape, 16, jnp.int32))


def kernel(
    d_out, combine, experts, slots, wg_hbm, wu_hbm, wd_hbm, sg_hbm, su_hbm,
    result,
    wg, wu, wd, sg, su, fac_g, fac_u, out, x1, zsend, arr, part_f, part, r1, u, xs, xr, dh, yp, yr, yown,
    gr, ret, snd, rx, pick, perm_out, perm_back, load_sem, send_sem, recv_sem,
):
    width = wd.shape[2]
    piece_w = width // 4
    node, local = lax.axis_index("node"), lax.axis_index("local")
    zh, j = lax.div(node, PEERS), lax.rem(node, PEERS)
    zl, y = lax.div(local, 4), lax.rem(local, 4)
    zq, zi = lax.div(zl, 4), lax.rem(zl, 4)

    def cols(start, size):
        return pl.ds(mul(start, 128), size)

    def peer(o):
        return {"node": zh * PEERS + lax.rem(j + o, PEERS), "local": local}

    def group(o):
        return {"node": lax.rem(zh + o, GROUPS) * PEERS + j, "local": local}

    def at_y(o):
        return {"node": node, "local": zl * 4 + lax.rem(y + o, 4)}

    def at_z(o):
        return {"node": node, "local": (zq * 4 + lax.rem(zi + o, 4)) * 4 + y}

    across = {"node": node, "local": ((1 - zq) * 4 + zi) * 4 + y}

    own = cols(y * width, width)
    loads = [
        pltpu.make_async_copy(src, dst, load_sem.at[i])
        for i, (src, dst) in enumerate((
            (wd_hbm.at[:, own], wd.at[y]), (sg_hbm.at[:, own], sg), (su_hbm.at[:, own], su),
            (wg_hbm.at[:, own], wg.at[y]), (wu_hbm.at[:, own], wu.at[y]),
        ))
    ]
    for load in loads:
        load.start()

    barrier = pltpu.get_barrier_semaphore()
    partners = [peer(o) for o in range(1, PEERS)] + [group(o) for o in range(1, GROUPS)]
    partners += [at_y(o) for o in range(1, 4)] + [at_z(o) for o in range(1, 4)] + [across]
    for partner in partners:
        pl.semaphore_signal(barrier, inc=1, device_id=partner, device_id_type=MESH)

    expert, number = experts[...], slots[...]
    eight, three = jnp.full(expert.shape, 3, jnp.int32), jnp.full(expert.shape, 3, jnp.int32)
    distance = lax.bitwise_and(lax.shift_right_logical(expert, eight) - zh + GROUPS, three)
    place = lax.bitwise_and(expert, jnp.full(expert.shape, 7, jnp.int32)) * PART + distance * CAP + number
    place = jnp.where(number >= 0, place, 2 * SLOTS)
    slot = lax.broadcasted_iota(jnp.int32, pick.shape, 0)
    chosen = jnp.zeros(slot.shape, F32)
    weight = jnp.zeros(slot.shape, F32)
    for k in range(3):
        hit = slot == place[k : k + 1, :]
        chosen = chosen + jnp.where(hit, 1.0, 0.0)
        weight = weight + jnp.where(hit, combine[k : k + 1, :], 0.0)
    pick[...] = chosen.astype(BF16)
    weight = jnp.sum(weight, axis=1, keepdims=True)
    out[...] = (contract(pick[...], d_out[...], 1) * weight).astype(BF16)

    row = lax.broadcasted_iota(jnp.int32, perm_out.shape, 0)
    col = lax.broadcasted_iota(jnp.int32, perm_out.shape, 1)
    d_of = by_const(row, 683)
    rest = row - d_of * ROWS
    j_of = by_const(rest, 5462)
    perm_out[...] = jnp.where(col == j_of * PART + d_of * CAP + rest - j_of * CAP, 1.0, 0.0).astype(BF16)

    pl.semaphore_wait(barrier, len(partners))

    started = []

    def send(src, dst, to):
        i = len(started)
        copy = pltpu.make_async_remote_copy(
            src_ref=src, dst_ref=dst, send_sem=send_sem.at[i], recv_sem=recv_sem.at[i], device_id=to, device_id_type=MESH,
        )
        copy.start()
        started.append(copy)
        return copy

    def piece(o):
        return pl.ds(mul(lax.rem(j + o, PEERS) * PART, 16), PART)

    def share(src, dst):
        return [send(src.at[:, cols(lax.rem(y + o, 4) * width, width)], dst.at[y], at_y(o)) for o in range(1, 4)]

    to_peers = [send(out.at[piece(o)], x1.at[piece(0)], peer(o)) for o in range(1, PEERS)]
    x1[piece(0), :] = out[piece(0), :]
    down = share(wd_hbm, wd)
    j_of = by_const(row, 1366)
    rest = row - j_of * PART
    d_of = by_const(rest, 5462)
    perm_back[...] = jnp.where(col == d_of * ROWS + j_of * CAP + rest - d_of * CAP, 1.0, 0.0).astype(BF16)
    for copy in to_peers:
        copy.wait_recv()
    sorted_rows = mat(perm_out[...], x1[...]).astype(BF16)
    to_groups = {}
    for d in ORDER[1:]:
        zsend[d] = sorted_rows[d * ROWS : (d + 1) * ROWS]
        to_groups[d] = send(zsend.at[d], arr.at[d, y], group(d))
    arr[0, y] = sorted_rows[:ROWS]

    pending = {}
    returned = []

    def stage(d, s):
        if s == 0:
            if d:
                to_groups[d].wait_recv()
            pending[d] = [send(arr.at[d, y], arr.at[d, y], at_y(o)) for o in range(1, 4)]
            if d == 0:
                pending["weights"] = share(wg_hbm, wg) + share(wu_hbm, wu)
                loads[1].wait()
                loads[2].wait()

                def factors(i, carry):
                    e = lax.div(i, ROWS // 16)
                    source = lax.rem(zh - e + GROUPS, GROUPS) * ROWS
                    inner = lax.rem(i, ROWS // 16) * 16
                    gate = sg[pl.ds(mul(source + inner, 16), 16), :].astype(F32)
                    up = su[pl.ds(mul(source + inner, 16), 16), :].astype(F32)
                    sig = 1.0 / (1.0 + jnp.exp(-gate))
                    to = pl.ds(mul(i * 16, 16), 16)
                    fac_g[to, :] = up * sig * (1.0 + gate * (1.0 - sig))
                    fac_u[to, :] = gate * sig
                    return carry

                lax.fori_loop(0, SLOTS // 16, factors, 0)
            return
        for copy in pending[d]:
            copy.wait_recv()
        if s == 1:
            if d == 0:
                loads[0].wait()
                for copy in down:
                    copy.wait_recv()
            total = mat(arr[d, 0], wd[0])
            for k in range(1, 4):
                total = total + mat(arr[d, k], wd[k])
            part_f[d] = total
            part[d] = total.astype(BF16)
            pending[d] = [
                send(part.at[d, :, cols(lax.rem(zi + o, 4) * piece_w, piece_w)], r1.at[d, o], at_z(o)) for o in range(1, 4)
            ]
        elif s == 2:
            total = part_f[d, :, cols(zi * piece_w, piece_w)]
            for o in range(1, 4):
                total = total + r1[d, o].astype(F32)
            xs[d] = total.astype(BF16)
            pending[d] = [send(xs.at[d], xr.at[d], across)]
            u[d] = total
        elif s == 3:
            c = cols(zi * piece_w, piece_w)
            dh[d, :, c] = (u[d] + xr[d].astype(F32)).astype(BF16)
            ref = dh.at[d, :, c]
            pending[d] = [send(ref, ref, at_z(o)) for o in range(1, 4)]
        elif s == 4:
            grad = dh[d].astype(F32)
            r = pl.ds(d * ROWS, ROWS)
            grad_gate = (grad * fac_g[r, :]).astype(BF16)
            grad_up = (grad * fac_u[r, :]).astype(BF16)
            if d == 0:
                loads[3].wait()
                loads[4].wait()
                for copy in pending["weights"]:
                    copy.wait_recv()
            pending[d] = []
            for o in (1, 2, 3, 0):
                k = lax.rem(y + o, 4)
                total = contract(grad_gate, wg[k], 1) + contract(grad_up, wu[k], 1)
                if o:
                    yp[d, o] = total.astype(BF16)
                    pending[d].append(send(yp.at[d, o], yr.at[d, o], at_y(o)))
                else:
                    yown[d] = total
        else:
            total = yown[d]
            for o in range(1, 4):
                total = total + yr[d, o].astype(F32)
            r = pl.ds(d * ROWS, ROWS)
            if d == 0:
                ret[r, :] = total.astype(BF16)
            else:
                gr[d] = total.astype(BF16)
                returned.append(send(gr.at[d], ret.at[r], group(GROUPS - d)))

    for t in range(max(LAG) + STAGES):
        for k, d in enumerate(ORDER):
            if 0 <= t - LAG[k] < STAGES:
                stage(d, t - LAG[k])

    for copy in returned:
        copy.wait_recv()
    snd[...] = mat(perm_back[...], ret[...]).astype(BF16)
    to_peers = [send(snd.at[piece(o)], rx.at[piece(0)], peer(o)) for o in range(1, PEERS)]
    rx[piece(0), :] = snd[piece(0), :]
    for copy in to_peers:
        copy.wait_recv()
    result[...] = contract(rx[...], pick[...], 0).astype(BF16)
    for copy in started:
        copy.wait_send()


def on_device(d_out, combine, expert_ids, slot_ids, w_gate, w_up, w_down, saved_gate, saved_up):
    feat, hid = w_gate.shape[1:]
    tokens = d_out.shape[0]
    w = hid // 4

    def two(*shape):
        return pltpu.VMEM(shape, BF16)

    def four(*shape):
        return pltpu.VMEM(shape, F32)

    vmem = pl.BlockSpec(memory_space=pltpu.VMEM)
    hbm = pl.BlockSpec(memory_space=pl.ANY)
    g = GROUPS
    return pl.pallas_call(
        kernel,
        out_shape=jax.ShapeDtypeStruct((feat, tokens), BF16),
        in_specs=[vmem] * 4 + [hbm] * 5,
        out_specs=vmem,
        scratch_shapes=[
            two(4, feat, w), two(4, feat, w), two(4, feat, w), two(SLOTS, w), two(SLOTS, w), four(SLOTS, w), four(SLOTS, w),
            two(SLOTS, feat), two(SLOTS, feat), two(g, ROWS, feat), two(g, 4, ROWS, feat),
            four(g, ROWS, w), two(g, ROWS, w), two(g, 4, ROWS, w // 4), four(g, ROWS, w // 4),
            two(g, ROWS, w // 4), two(g, ROWS, w // 4), two(g, ROWS, w),
            two(g, 4, ROWS, feat), two(g, 4, ROWS, feat), four(g, ROWS, feat),
            two(g, ROWS, feat), two(SLOTS, feat), two(SLOTS, feat), two(SLOTS, feat),
            two(SLOTS, tokens), two(SLOTS, SLOTS), two(SLOTS, SLOTS),
            pltpu.SemaphoreType.DMA((5,)), pltpu.SemaphoreType.DMA((NCOPY,)), pltpu.SemaphoreType.DMA((NCOPY,)),
        ],
        compiler_params=pltpu.CompilerParams(
            collective_id=0, has_side_effects=True, vmem_limit_bytes=60 * 1024 * 1024
        ),
        cost_estimate=pl.CostEstimate(flops=1_200_000_000, bytes_accessed=8_000_000, transcendentals=800_000),
    )(
        d_out.T, combine.T, expert_ids.T, slot_ids.T,
        w_gate[0], w_up[0], w_down[0].T, saved_gate[0], saved_up[0],
    ).T


def solution(mesh):
    return jax.shard_map(
        on_device,
        mesh=mesh,
        in_specs=(
            P("node", "local"), P("node", None), P("node", None), P("node", None),
            P("node", "local", None), P("node", "local", None), P("node", None, "local"),
            P("node", None, None), P("node", None, None),
        ),
        out_specs=P("node", "local"),
        check_vma=False,
    )
```

```python
import jax
import jax.numpy as jnp
from jax import lax
from jax.experimental import pallas as pl
from jax.experimental.pallas import tpu as pltpu
from jax.sharding import PartitionSpec as P

F32, BF16 = jnp.float32, jnp.bfloat16
GROUPS, PEERS, CAP = 4, 8, 12
ROWS = PEERS * CAP
PART = GROUPS * CAP
SLOTS = GROUPS * ROWS
ORDER = (0, 1, 3, 2)
LAG = (0, 3, 3, 3)
STAGES = 6
FIRST = 1
HOLD = 6
NCOPY = 2 * 7 + 2 * 3 + 3 * 3 + GROUPS * 13
MESH = pl.DeviceIdType.MESH


def mul(value, unit):
    return pl.multiple_of(value, unit)


def mat(a, b):
    return jnp.dot(a, b, preferred_element_type=F32)


def contract(a, b, dim):
    return lax.dot_general(a, b, (((dim,), (dim,)), ((), ())), preferred_element_type=F32)


def by_const(value, factor):
    return lax.shift_right_logical(value * factor, jnp.full(value.shape, 16, jnp.int32))


def kernel(
    d_out, combine, experts, slots, wg_hbm, wu_hbm, wd_hbm, sg_hbm, su_hbm,
    result,
    wg, wu, wd, sg, su, fac_g, fac_u, out, x1, zsend, arr, part_f, part, r1, u, xs, xr, dh, yp, yr, yown,
    gr, ret, snd, rx, pick, perm_out, perm_back, load_sem, send_sem, recv_sem, far_sem,
):
    width = wd.shape[2]
    piece_w = width // 4
    node, local = lax.axis_index("node"), lax.axis_index("local")
    zh, j = lax.div(node, PEERS), lax.rem(node, PEERS)
    zl, y = lax.div(local, 4), lax.rem(local, 4)
    zq, zi = lax.div(zl, 4), lax.rem(zl, 4)

    def cols(start, size):
        return pl.ds(mul(start, 128), size)

    def peer(o):
        return {"node": zh * PEERS + lax.rem(j + o, PEERS), "local": local}

    def group(o):
        return {"node": lax.rem(zh + o, GROUPS) * PEERS + j, "local": local}

    def at_y(o):
        return {"node": node, "local": zl * 4 + lax.rem(y + o, 4)}

    def at_z(o):
        return {"node": node, "local": (zq * 4 + lax.rem(zi + o, 4)) * 4 + y}

    across = {"node": node, "local": ((1 - zq) * 4 + zi) * 4 + y}

    own = cols(y * width, width)
    loads = [
        pltpu.make_async_copy(src, dst, load_sem.at[i])
        for i, (src, dst) in enumerate((
            (wd_hbm.at[:, own], wd.at[y]), (sg_hbm.at[:, own], sg), (su_hbm.at[:, own], su),
            (wg_hbm.at[:, own], wg.at[y]), (wu_hbm.at[:, own], wu.at[y]),
        ))
    ]
    for load in loads:
        load.start()

    barrier = pltpu.get_barrier_semaphore()
    partners = [peer(o) for o in range(1, PEERS)] + [group(1), group(3)]
    partners += [at_y(o) for o in range(1, 4)] + [at_z(o) for o in range(1, 4)] + [across]
    for partner in partners:
        pl.semaphore_signal(barrier, inc=1, device_id=partner, device_id_type=MESH)

    expert, number = experts[...], slots[...]
    eight, three = jnp.full(expert.shape, 3, jnp.int32), jnp.full(expert.shape, 3, jnp.int32)
    distance = lax.bitwise_and(lax.shift_right_logical(expert, eight) - zh + GROUPS, three)
    place = lax.bitwise_and(expert, jnp.full(expert.shape, 7, jnp.int32)) * PART + distance * CAP + number
    place = jnp.where(number >= 0, place, 2 * SLOTS)
    slot = lax.broadcasted_iota(jnp.int32, pick.shape, 0)
    chosen = jnp.zeros(slot.shape, F32)
    weight = jnp.zeros(slot.shape, F32)
    for k in range(3):
        hit = slot == place[k : k + 1, :]
        chosen = chosen + jnp.where(hit, 1.0, 0.0)
        weight = weight + jnp.where(hit, combine[k : k + 1, :], 0.0)
    pick[...] = chosen.astype(BF16)
    weight = jnp.sum(weight, axis=1, keepdims=True)
    out[...] = (contract(pick[...], d_out[...], 1) * weight).astype(BF16)

    row = lax.broadcasted_iota(jnp.int32, perm_out.shape, 0)
    col = lax.broadcasted_iota(jnp.int32, perm_out.shape, 1)
    d_of = by_const(row, 683)
    rest = row - d_of * ROWS
    j_of = by_const(rest, 5462)
    perm_out[...] = jnp.where(col == j_of * PART + d_of * CAP + rest - j_of * CAP, 1.0, 0.0).astype(BF16)

    pl.semaphore_wait(barrier, len(partners))
    for o in (1, 3):
        pl.semaphore_signal(far_sem.at[o], inc=1, device_id=group(o), device_id_type=MESH)

    started = []

    def send(src, dst, to):
        i = len(started)
        copy = pltpu.make_async_remote_copy(
            src_ref=src, dst_ref=dst, send_sem=send_sem.at[i], recv_sem=recv_sem.at[i], device_id=to, device_id_type=MESH,
        )
        copy.start()
        started.append(copy)
        return copy

    def piece(o):
        return pl.ds(mul(lax.rem(j + o, PEERS) * PART, 16), PART)

    def share(src, dst):
        return [send(src.at[:, cols(lax.rem(y + o, 4) * width, width)], dst.at[y], at_y(o)) for o in range(1, 4)]

    to_peers = [send(out.at[piece(o)], x1.at[piece(0)], peer(o)) for o in range(1, PEERS)]
    x1[piece(0), :] = out[piece(0), :]
    down = share(wd_hbm, wd)
    j_of = by_const(row, 1366)
    rest = row - j_of * PART
    d_of = by_const(rest, 5462)
    perm_back[...] = jnp.where(col == d_of * ROWS + j_of * CAP + rest - d_of * CAP, 1.0, 0.0).astype(BF16)
    for copy in to_peers:
        copy.wait_recv()
    sorted_rows = mat(perm_out[...], x1[...]).astype(BF16)
    to_groups = {}
    for d in ORDER[1:]:
        zsend[d] = sorted_rows[d * ROWS : (d + 1) * ROWS]
        if d == 2:
            for o in (1, 3):
                pl.semaphore_wait(far_sem.at[o], 1)
        to_groups[d] = send(zsend.at[d], arr.at[d, y], group(d))
    arr[0, y] = sorted_rows[:ROWS]

    pending = {}
    returned = []

    def stage(d, s):
        if s == 0:
            if d:
                to_groups[d].wait_recv()
            pending[d] = [send(arr.at[d, y], arr.at[d, y], at_y(o)) for o in range(1, 4)]
            if d == 0:
                pending["weights"] = share(wg_hbm, wg) + share(wu_hbm, wu)
                loads[1].wait()
                loads[2].wait()

                def factors(i, carry):
                    e = lax.div(i, ROWS // 16)
                    source = lax.rem(zh - e + GROUPS, GROUPS) * ROWS
                    inner = lax.rem(i, ROWS // 16) * 16
                    gate = sg[pl.ds(mul(source + inner, 16), 16), :].astype(F32)
                    up = su[pl.ds(mul(source + inner, 16), 16), :].astype(F32)
                    sig = 1.0 / (1.0 + jnp.exp(-gate))
                    to = pl.ds(mul(i * 16, 16), 16)
                    fac_g[to, :] = up * sig * (1.0 + gate * (1.0 - sig))
                    fac_u[to, :] = gate * sig
                    return carry

                lax.fori_loop(0, SLOTS // 16, factors, 0)
            return
        for copy in pending[d]:
            copy.wait_recv()
        if s == 1:
            if d == 0:
                loads[0].wait()
                for copy in down:
                    copy.wait_recv()
            total = mat(arr[d, 0], wd[0])
            for k in range(1, 4):
                total = total + mat(arr[d, k], wd[k])
            part_f[d] = total
            part[d] = total.astype(BF16)
            pending[d] = [
                send(part.at[d, :, cols(lax.rem(zi + o, 4) * piece_w, piece_w)], r1.at[d, o], at_z(o)) for o in range(1, 4)
            ]
        elif s == 2:
            total = part_f[d, :, cols(zi * piece_w, piece_w)]
            for o in range(1, 4):
                total = total + r1[d, o].astype(F32)
            xs[d] = total.astype(BF16)
            pending[d] = [send(xs.at[d], xr.at[d], across)]
            u[d] = total
        elif s == 3:
            c = cols(zi * piece_w, piece_w)
            dh[d, :, c] = (u[d] + xr[d].astype(F32)).astype(BF16)
            ref = dh.at[d, :, c]
            pending[d] = [send(ref, ref, at_z(o)) for o in range(1, 4)]
        elif s == 4:
            grad = dh[d].astype(F32)
            r = pl.ds(d * ROWS, ROWS)
            grad_gate = (grad * fac_g[r, :]).astype(BF16)
            grad_up = (grad * fac_u[r, :]).astype(BF16)
            if d == FIRST:
                loads[3].wait()
                loads[4].wait()
                for copy in pending["weights"]:
                    copy.wait_recv()
            pending[d] = []
            for o in (1, 2, 3, 0):
                k = lax.rem(y + o, 4)
                total = contract(grad_gate, wg[k], 1) + contract(grad_up, wu[k], 1)
                if o:
                    yp[d, o] = total.astype(BF16)
                    pending[d].append(send(yp.at[d, o], yr.at[d, o], at_y(o)))
                else:
                    yown[d] = total
        else:
            total = yown[d]
            for o in range(1, 4):
                total = total + yr[d, o].astype(F32)
            r = pl.ds(d * ROWS, ROWS)
            if d == 0:
                ret[r, :] = total.astype(BF16)
            else:
                gr[d] = total.astype(BF16)
                returned.append(send(gr.at[d], ret.at[r], group(GROUPS - d)))

    work = [(s + LAG[k] + (HOLD if d == 0 and s >= 4 else 0), k, d, s) for k, d in enumerate(ORDER) for s in range(STAGES)]
    for _, _, d, s in sorted(work):
        stage(d, s)

    for copy in returned:
        copy.wait_recv()
    snd[...] = mat(perm_back[...], ret[...]).astype(BF16)
    to_peers = [send(snd.at[piece(o)], rx.at[piece(0)], peer(o)) for o in range(1, PEERS)]
    rx[piece(0), :] = snd[piece(0), :]
    for copy in to_peers:
        copy.wait_recv()
    result[...] = contract(rx[...], pick[...], 0).astype(BF16)
    for copy in started:
        copy.wait_send()


def on_device(d_out, combine, expert_ids, slot_ids, w_gate, w_up, w_down, saved_gate, saved_up):
    feat, hid = w_gate.shape[1:]
    tokens = d_out.shape[0]
    w = hid // 4

    def two(*shape):
        return pltpu.VMEM(shape, BF16)

    def four(*shape):
        return pltpu.VMEM(shape, F32)

    vmem = pl.BlockSpec(memory_space=pltpu.VMEM)
    hbm = pl.BlockSpec(memory_space=pl.ANY)
    g = GROUPS
    return pl.pallas_call(
        kernel,
        out_shape=jax.ShapeDtypeStruct((feat, tokens), BF16),
        in_specs=[vmem] * 4 + [hbm] * 5,
        out_specs=vmem,
        scratch_shapes=[
            two(4, feat, w), two(4, feat, w), two(4, feat, w), two(SLOTS, w), two(SLOTS, w), four(SLOTS, w), four(SLOTS, w),
            two(SLOTS, feat), two(SLOTS, feat), two(g, ROWS, feat), two(g, 4, ROWS, feat),
            four(g, ROWS, w), two(g, ROWS, w), two(g, 4, ROWS, w // 4), four(g, ROWS, w // 4),
            two(g, ROWS, w // 4), two(g, ROWS, w // 4), two(g, ROWS, w),
            two(g, 4, ROWS, feat), two(g, 4, ROWS, feat), four(g, ROWS, feat),
            two(g, ROWS, feat), two(SLOTS, feat), two(SLOTS, feat), two(SLOTS, feat),
            two(SLOTS, tokens), two(SLOTS, SLOTS), two(SLOTS, SLOTS),
            pltpu.SemaphoreType.DMA((5,)), pltpu.SemaphoreType.DMA((NCOPY,)), pltpu.SemaphoreType.DMA((NCOPY,)),
            pltpu.SemaphoreType.REGULAR((4,)),
        ],
        compiler_params=pltpu.CompilerParams(
            collective_id=0, has_side_effects=True, vmem_limit_bytes=60 * 1024 * 1024
        ),
        cost_estimate=pl.CostEstimate(flops=1_200_000_000, bytes_accessed=8_000_000, transcendentals=800_000),
    )(
        d_out.T, combine.T, expert_ids.T, slot_ids.T,
        w_gate[0], w_up[0], w_down[0].T, saved_gate[0], saved_up[0],
    ).T


def solution(mesh):
    return jax.shard_map(
        on_device,
        mesh=mesh,
        in_specs=(
            P("node", "local"), P("node", None), P("node", None), P("node", None),
            P("node", "local", None), P("node", "local", None), P("node", None, "local"),
            P("node", None, None), P("node", None, None),
        ),
        out_specs=P("node", "local"),
        check_vma=False,
    )
```

```python
import jax
import jax.numpy as jnp
from jax import lax
from jax.experimental import pallas as pl
from jax.experimental.pallas import tpu as pltpu
from jax.sharding import PartitionSpec as P

F32, BF16 = jnp.float32, jnp.bfloat16
GROUPS, PEERS, CAP = 4, 8, 12
ROWS = PEERS * CAP
PART = GROUPS * CAP
SLOTS = GROUPS * ROWS
CHUNKS = ((0, 0, 96), (2, 0, 96), (1, 0, 96), (3, 0, 96))
LAG = (0, 3, 3, 3)
STAGES = 6
HOLD = 6
FIRST = 1
NCOPY = 2 * 7 + 3 * 3 + len(CHUNKS) * 15
MESH = pl.DeviceIdType.MESH


def mul(value, unit):
    return pl.multiple_of(value, unit)


def mat(a, b):
    return jnp.dot(a, b, preferred_element_type=F32)


def contract(a, b, dim):
    return lax.dot_general(a, b, (((dim,), (dim,)), ((), ())), preferred_element_type=F32)


def by_const(value, factor):
    return lax.shift_right_logical(value * factor, jnp.full(value.shape, 16, jnp.int32))


def kernel(
    d_out, combine, experts, slots, wg_hbm, wu_hbm, wd_hbm, sg_hbm, su_hbm,
    result,
    wg, wu, wd, sg, su, fac_g, fac_u, out, x1, zsend, arr, part_f, part, r1, u, xs, xr, dh, yp, yr, yown,
    gr, ret, snd, rx, pick, perm_out, perm_back, wd_all, wg_all, wu_all, load_sem, send_sem, recv_sem, far_sem,
):
    width = wd.shape[2]
    piece_w = width // 4
    node, local = lax.axis_index("node"), lax.axis_index("local")
    zh, j = lax.div(node, PEERS), lax.rem(node, PEERS)
    zl, y = lax.div(local, 4), lax.rem(local, 4)
    zq, zi = lax.div(zl, 4), lax.rem(zl, 4)

    def cols(start, size):
        return pl.ds(mul(start, 128), size)

    def peer(o):
        return {"node": zh * PEERS + lax.rem(j + o, PEERS), "local": local}

    def group(o):
        return {"node": lax.rem(zh + o, GROUPS) * PEERS + j, "local": local}

    def at_y(o):
        return {"node": node, "local": zl * 4 + lax.rem(y + o, 4)}

    def at_z(o):
        return {"node": node, "local": (zq * 4 + lax.rem(zi + o, 4)) * 4 + y}

    across = {"node": node, "local": ((1 - zq) * 4 + zi) * 4 + y}

    own = cols(y * width, width)
    loads = [
        pltpu.make_async_copy(src, dst, load_sem.at[i])
        for i, (src, dst) in enumerate((
            (wd_hbm.at[:, own], wd.at[y]), (sg_hbm.at[:, own], sg), (su_hbm.at[:, own], su),
            (wg_hbm.at[:, own], wg.at[y]), (wu_hbm.at[:, own], wu.at[y]),
            (wd_hbm, wd_all), (wg_hbm, wg_all), (wu_hbm, wu_all),
        ))
    ]
    for load in loads:
        load.start()

    barrier = pltpu.get_barrier_semaphore()
    partners = [peer(o) for o in range(1, PEERS)] + [group(1), group(3)]
    partners += [at_y(o) for o in range(1, 4)] + [at_z(o) for o in range(1, 4)] + [across]
    for partner in partners:
        pl.semaphore_signal(barrier, inc=1, device_id=partner, device_id_type=MESH)

    expert, number = experts[...], slots[...]
    eight, three = jnp.full(expert.shape, 3, jnp.int32), jnp.full(expert.shape, 3, jnp.int32)
    distance = lax.bitwise_and(lax.shift_right_logical(expert, eight) - zh + GROUPS, three)
    place = lax.bitwise_and(expert, jnp.full(expert.shape, 7, jnp.int32)) * PART + distance * CAP + number
    place = jnp.where(number >= 0, place, 2 * SLOTS)
    slot = lax.broadcasted_iota(jnp.int32, pick.shape, 0)
    chosen = jnp.zeros(slot.shape, F32)
    weight = jnp.zeros(slot.shape, F32)
    for k in range(3):
        hit = slot == place[k : k + 1, :]
        chosen = chosen + jnp.where(hit, 1.0, 0.0)
        weight = weight + jnp.where(hit, combine[k : k + 1, :], 0.0)
    pick[...] = chosen.astype(BF16)
    weight = jnp.sum(weight, axis=1, keepdims=True)
    out[...] = (contract(pick[...], d_out[...], 1) * weight).astype(BF16)

    row = lax.broadcasted_iota(jnp.int32, perm_out.shape, 0)
    col = lax.broadcasted_iota(jnp.int32, perm_out.shape, 1)
    d_of = by_const(row, 683)
    rest = row - d_of * ROWS
    j_of = by_const(rest, 5462)
    perm_out[...] = jnp.where(col == j_of * PART + d_of * CAP + rest - j_of * CAP, 1.0, 0.0).astype(BF16)

    pl.semaphore_wait(barrier, len(partners))
    for o in (1, 3):
        pl.semaphore_signal(far_sem.at[o], inc=1, device_id=group(o), device_id_type=MESH)

    started = []

    def send(src, dst, to):
        i = len(started)
        copy = pltpu.make_async_remote_copy(
            src_ref=src, dst_ref=dst, send_sem=send_sem.at[i], recv_sem=recv_sem.at[i], device_id=to, device_id_type=MESH,
        )
        copy.start()
        started.append(copy)
        return copy

    def piece(o):
        return pl.ds(mul(lax.rem(j + o, PEERS) * PART, 16), PART)

    def share(src, dst):
        return [send(src.at[:, cols(lax.rem(y + o, 4) * width, width)], dst.at[y], at_y(o)) for o in range(1, 4)]

    to_peers = [send(out.at[piece(o)], x1.at[piece(0)], peer(o)) for o in range(1, PEERS)]
    x1[piece(0), :] = out[piece(0), :]
    loads[5].wait()
    down = share(wd_all, wd)
    j_of = by_const(row, 1366)
    rest = row - j_of * PART
    d_of = by_const(rest, 5462)
    perm_back[...] = jnp.where(col == d_of * ROWS + j_of * CAP + rest - d_of * CAP, 1.0, 0.0).astype(BF16)
    for copy in to_peers:
        copy.wait_recv()
    sorted_rows = mat(perm_out[...], x1[...]).astype(BF16)
    to_groups = {}
    zsend[...] = sorted_rows
    arr[y, 0:ROWS, :] = sorted_rows[:ROWS]
    far = True
    for n, (d, low, count) in enumerate(CHUNKS):
        if d == 2 and far:
            far = False
            for o in (1, 3):
                pl.semaphore_wait(far_sem.at[o], 1)
        if d:
            r = pl.ds(d * ROWS + low, count)
            to_groups[n] = send(zsend.at[r], arr.at[y, r], group(d))

    pending = {}
    returned = []

    def stage(n, s):
        d, low, count = CHUNKS[n]
        r = pl.ds(d * ROWS + low, count)
        if s == 0:
            if d:
                to_groups[n].wait_recv()
            pending[n] = [send(arr.at[y, r], arr.at[y, r], at_y(o)) for o in range(1, 4)]
            if n == 0:
                loads[6].wait()
                loads[7].wait()
                pending["weights"] = share(wg_all, wg) + share(wu_all, wu)
                loads[1].wait()
                loads[2].wait()

                def factors(i, carry):
                    e = lax.div(i, ROWS // 16)
                    source = lax.rem(zh - e + GROUPS, GROUPS) * ROWS
                    inner = lax.rem(i, ROWS // 16) * 16
                    gate = sg[pl.ds(mul(source + inner, 16), 16), :].astype(F32)
                    up = su[pl.ds(mul(source + inner, 16), 16), :].astype(F32)
                    sig = 1.0 / (1.0 + jnp.exp(-gate))
                    to = pl.ds(mul(i * 16, 16), 16)
                    fac_g[to, :] = up * sig * (1.0 + gate * (1.0 - sig))
                    fac_u[to, :] = gate * sig
                    return carry

                lax.fori_loop(0, SLOTS // 16, factors, 0)
            return
        for copy in pending[n]:
            copy.wait_recv()
        if s == 1:
            if n == 0:
                loads[0].wait()
                for copy in down:
                    copy.wait_recv()
            total = mat(arr[0, r, :], wd[0])
            for k in range(1, 4):
                total = total + mat(arr[k, r, :], wd[k])
            part_f[r, :] = total
            part[r, :] = total.astype(BF16)
            pending[n] = [
                send(part.at[r, cols(lax.rem(zi + o, 4) * piece_w, piece_w)], r1.at[o, r], at_z(o)) for o in range(1, 4)
            ]
        elif s == 2:
            total = part_f[r, cols(zi * piece_w, piece_w)]
            for o in range(1, 4):
                total = total + r1[o, r, :].astype(F32)
            xs[r, :] = total.astype(BF16)
            pending[n] = [send(xs.at[r], xr.at[r], across)]
            u[r, :] = total
        elif s == 3:
            c = cols(zi * piece_w, piece_w)
            dh[r, c] = (u[r, :] + xr[r, :].astype(F32)).astype(BF16)
            ref = dh.at[r, c]
            pending[n] = [send(ref, ref, at_z(o)) for o in range(1, 4)]
        elif s == 4:
            grad = dh[r, :].astype(F32)
            grad_gate = (grad * fac_g[r, :]).astype(BF16)
            grad_up = (grad * fac_u[r, :]).astype(BF16)
            if n == FIRST:
                loads[3].wait()
                loads[4].wait()
                for copy in pending["weights"]:
                    copy.wait_recv()
            pending[n] = []
            for o in (1, 2, 3, 0):
                k = lax.rem(y + o, 4)
                total = contract(grad_gate, wg[k], 1) + contract(grad_up, wu[k], 1)
                if o:
                    yp[o, r, :] = total.astype(BF16)
                    pending[n].append(send(yp.at[o, r], yr.at[o, r], at_y(o)))
                else:
                    yown[r, :] = total
        else:
            total = yown[r, :]
            for o in range(1, 4):
                total = total + yr[o, r, :].astype(F32)
            if n == 0:
                ret[r, :] = total.astype(BF16)
            else:
                gr[r, :] = total.astype(BF16)
                returned.append(send(gr.at[r], ret.at[r], group(GROUPS - d)))

    work = [(s + LAG[n] + (HOLD if n == 0 and s >= 4 else 0), n, s) for n in range(len(CHUNKS)) for s in range(STAGES)]
    for _, n, s in sorted(work):
        stage(n, s)

    for copy in returned:
        copy.wait_recv()
    snd[...] = mat(perm_back[...], ret[...]).astype(BF16)
    to_peers = [send(snd.at[piece(o)], rx.at[piece(0)], peer(o)) for o in range(1, PEERS)]
    rx[piece(0), :] = snd[piece(0), :]
    for copy in to_peers:
        copy.wait_recv()
    result[...] = contract(rx[...], pick[...], 0).astype(BF16)
    for copy in started:
        copy.wait_send()


def on_device(d_out, combine, expert_ids, slot_ids, w_gate, w_up, w_down, saved_gate, saved_up):
    feat, hid = w_gate.shape[1:]
    tokens = d_out.shape[0]
    w = hid // 4

    def two(*shape):
        return pltpu.VMEM(shape, BF16)

    def four(*shape):
        return pltpu.VMEM(shape, F32)

    vmem = pl.BlockSpec(memory_space=pltpu.VMEM)
    hbm = pl.BlockSpec(memory_space=pl.ANY)
    return pl.pallas_call(
        kernel,
        out_shape=jax.ShapeDtypeStruct((feat, tokens), BF16),
        in_specs=[vmem] * 4 + [hbm] * 5,
        out_specs=vmem,
        scratch_shapes=[
            two(4, feat, w), two(4, feat, w), two(4, feat, w), two(SLOTS, w), two(SLOTS, w), four(SLOTS, w), four(SLOTS, w),
            two(SLOTS, feat), two(SLOTS, feat), two(SLOTS, feat), two(4, SLOTS, feat),
            four(SLOTS, w), two(SLOTS, w), two(4, SLOTS, w // 4), four(SLOTS, w // 4),
            two(SLOTS, w // 4), two(SLOTS, w // 4), two(SLOTS, w),
            two(4, SLOTS, feat), two(4, SLOTS, feat), four(SLOTS, feat),
            two(SLOTS, feat), two(SLOTS, feat), two(SLOTS, feat), two(SLOTS, feat),
            two(SLOTS, tokens), two(SLOTS, SLOTS), two(SLOTS, SLOTS),
            two(feat, hid), two(feat, hid), two(feat, hid),
            pltpu.SemaphoreType.DMA((8,)), pltpu.SemaphoreType.DMA((NCOPY,)), pltpu.SemaphoreType.DMA((NCOPY,)),
            pltpu.SemaphoreType.REGULAR((4,)),
        ],
        compiler_params=pltpu.CompilerParams(
            collective_id=0, has_side_effects=True, vmem_limit_bytes=60 * 1024 * 1024
        ),
        cost_estimate=pl.CostEstimate(flops=1_200_000_000, bytes_accessed=8_000_000, transcendentals=800_000),
    )(
        d_out.T, combine.T, expert_ids.T, slot_ids.T,
        w_gate[0], w_up[0], w_down[0].T, saved_gate[0], saved_up[0],
    ).T


def solution(mesh):
    return jax.shard_map(
        on_device,
        mesh=mesh,
        in_specs=(
            P("node", "local"), P("node", None), P("node", None), P("node", None),
            P("node", "local", None), P("node", "local", None), P("node", None, "local"),
            P("node", None, None), P("node", None, None),
        ),
        out_specs=P("node", "local"),
        check_vma=False,
    )
```
